512 devices in a mesh: expert: 64 (over z_lo, y, core), dp: 8 (over z_hi, x).
Axes of the slice: x: 4, y: 4, z: 16 (z_hi: 2, z_lo: 8; z = z_hi * 8 + z_lo), core: 2. Of those that a mesh axis runs over, the one named last changes fastest.
Arguments:
- tokens_one: bfloat16 [1536, 4096], P('expert', 'dp'), may hold values from -6 to 6
- gates_one: float32 [1536, 8], P('expert'), may hold values from 0.05 to 1
- experts_one: int32 [1536, 8], P('expert'), may hold values from 0 to 63, all different within a row; in each aligned block of 24 rows (0 to 23, 24 to 47, ...) at most 6 rows name the same one
- tokens_two: bfloat16 [1536, 4096], P('expert', 'dp'), may hold values from -6 to 6
- gates_two: float32 [1536, 8], P('expert'), may hold values from 0.05 to 1
- experts_two: int32 [1536, 8], P('expert'), may hold values from 0 to 63, all different within a row; in each aligned block of 24 rows (0 to 23, 24 to 47, ...) at most 6 rows name the same one
- gate_weight: bfloat16 [64, 1536, 4096], P('expert', 'dp'), may hold values from -0.09375 to 0.09375
- up_weight: bfloat16 [64, 1536, 4096], P('expert', 'dp'), may hold values from -0.09375 to 0.09375
- down_weight: bfloat16 [64, 1536, 4096], P('expert', None, 'dp'), may hold values from -0.15625 to 0.15625
Outputs:
- mixed_one: bfloat16 [1536, 4096], P('expert', 'dp')
- mixed_two: bfloat16 [1536, 4096], P('expert', 'dp')
The draws below stay inside these ranges and needn't reach their ends.
Inputs may be any that keep to these rules, and one draw needn't show every extreme that they name: `experts_one`: within the rows of one device (24 tokens, aligned blocks) no expert is picked more than 6 times, and each token picks 8 different experts. `experts_two`: within the rows of one device (24 tokens, aligned blocks) no expert is picked more than 6 times, and each token picks 8 different experts.
All inputs are finite; a program needn't handle non-finite values.
Results may differ from the reference program's by a relative error of at most 0.0057.
Values may be sent and summed in bfloat16 or wider, within the bound.
A program may use at most 64 MiB of HBM per device.

```python
import math
import jax
import jax.numpy as jnp
import numpy as np
from jax import lax

D = 4096
H = 1536
TOPK = 8
TOK_DEV = 24
EXPERTS = 64
TOKENS = 1536
CAP = 6


def shard_levels(key, shape, pieces, smallest, top_value):
    def one(axis_at, shards_of):
        heights = jax.random.uniform(jax.random.fold_in(jax.random.fold_in(key, 6), axis_at), (shards_of,), jnp.float32, smallest / len(pieces), top_value / len(pieces))
        return jnp.repeat(jnp.exp(heights), shape[axis_at] // shards_of).reshape((-1,) + (1,) * (len(shape) - axis_at - 1))

    loudness = one(*pieces[0])
    for cut in pieces[1:]:
        loudness = loudness * one(*cut)
    return loudness


def shared_out(key, own, number, rows, count, top, limit, slope):
    sequence = jax.random.permutation(key, count)
    crowded, common = portions_of(count, rows * top, limit, slope, True), portions_of(count, rows * top, limit, slope, False)
    places = jnp.arange(count)

    def named(sizes, turn):
        used = int((sizes > 0).sum())
        fixed = max(1, used // 4)
        shifted = fixed + (places - fixed + turn * (used - fixed)) % max(1, count - fixed)
        return jnp.zeros((count,), jnp.int32).at[sequence[jnp.where(places < fixed, places, shifted)]].set(jnp.asarray(sizes, jnp.int32))

    sizes = jnp.where(number % 4 == 0, named(crowded, number // 4), named(common, number - number // 4 - 1))
    mixed = jax.random.permutation(jax.random.fold_in(own, 3), count)
    source_of, sink = mixed[0:count // 2 * 2:2], mixed[1:count // 2 * 2:2]
    room = jnp.minimum(sizes[source_of] - 1, limit - sizes[sink]) // 2
    room = jnp.where((source_of == sequence[0]) | (sink == sequence[0]) | (sizes[sink] == 0), 0, jnp.maximum(room, 0))
    shifted = jax.random.randint(jax.random.fold_in(own, 4), (count // 2,), 0, 1 << 20) % (room + 1)
    sizes = sizes.at[source_of].add(-shifted).at[sink].add(shifted)
    items = jnp.searchsorted(jnp.cumsum(sizes), jnp.arange(rows * top), side="right").astype(jnp.int32)
    table = items.reshape(top, rows).T
    table = table[jax.random.permutation(jax.random.fold_in(own, 1), rows)]
    turn = jax.random.randint(jax.random.fold_in(own, 2), (rows, 1), 0, top)
    return jnp.take_along_axis(table, (jnp.arange(top)[None, :] + turn) % top, axis=1)


def portions_of(number_of, total, limit, skew, full):
    loads = [(1 << 20) // math.isqrt(rank ** skew) + 1 for rank in range(1, number_of + 1)]
    largest = limit if full else min(limit, max(-(-total // number_of), total * loads[0] // sum(loads)))
    least = 1 if total - largest >= number_of - 1 else 0
    given, surplus = [largest] + [least] * (number_of - 1), total - largest - least * (number_of - 1)
    while surplus > 0:
        candidates = [i for i in range(1, number_of) if given[i] < largest] or [i for i in range(1, number_of) if given[i] < limit]
        pool, remaining = sum([loads[i] for i in candidates]), surplus
        for i in candidates:
            more = min(limit - given[i], max(1, remaining * loads[i] // pool), surplus)
            given[i] = given[i] + more
            surplus = surplus - more
    return np.array(given)


def gaussian(key, dims, spread, most, shards=(), held_as=jnp.bfloat16):
    values = jax.random.normal(key, dims, jnp.float32) * spread
    if len(shards) > 0:
        values = shard_levels(key, dims, shards, -0.22, 0.18) * values
    return jnp.clip(values, min=-most, max=most).astype(held_as)


def setup_inputs(seed: int = 0) -> dict:
    arg_keys = jax.random.split(jax.random.key(seed), 10)
    tokens_one = gaussian(arg_keys[0], (TOKENS, D), 1.0, 6.0, ((0, 64), (1, 8)))
    gates_one = jnp.clip(jnp.exp(math.log(1.0) - 2.9957323 * jax.random.uniform(arg_keys[1], (TOKENS, TOPK), jnp.float32) ** shard_levels(arg_keys[1], (TOKENS, TOPK), ((0, 64),), -0.2, 0.2)), 0.05, 1.0)
    experts_one_keys = jax.random.split(jax.random.fold_in(arg_keys[2], 1), TOKENS // TOK_DEV)
    experts_one_turns = jax.random.permutation(jax.random.fold_in(arg_keys[2], 3), TOKENS // TOK_DEV)
    experts_one = jax.vmap(lambda own, number: shared_out(jax.random.fold_in(arg_keys[2], 2), own, number, TOK_DEV, EXPERTS, TOPK, CAP, 2))(experts_one_keys, experts_one_turns).reshape((TOKENS, TOPK))
    tokens_two = gaussian(arg_keys[3], (TOKENS, D), 1.0, 6.0, ((0, 64), (1, 8)))
    gates_two = jnp.clip(jnp.exp(math.log(1.0) - 2.9957323 * jax.random.uniform(arg_keys[4], (TOKENS, TOPK), jnp.float32) ** shard_levels(arg_keys[4], (TOKENS, TOPK), ((0, 64),), -0.2, 0.2)), 0.05, 1.0)
    experts_two_keys = jax.random.split(jax.random.fold_in(arg_keys[5], 1), TOKENS // TOK_DEV)
    experts_two_turns = jax.random.permutation(jax.random.fold_in(arg_keys[5], 3), TOKENS // TOK_DEV)
    experts_two = jax.vmap(lambda own, number: shared_out(jax.random.fold_in(arg_keys[5], 2), own, number, TOK_DEV, EXPERTS, TOPK, CAP, 2))(experts_two_keys, experts_two_turns).reshape((TOKENS, TOPK))
    gate_weight = gaussian(arg_keys[6], (EXPERTS, H, D), D ** -0.5, 0.09375, ((0, 64), (1, 8)))
    up_weight = gaussian(arg_keys[7], (EXPERTS, H, D), D ** -0.5, 0.09375, ((0, 64), (1, 8)))
    down_weight = gaussian(arg_keys[8], (EXPERTS, H, D), H ** -0.5, 0.15625, ((0, 64), (2, 8)))
    return dict(tokens_one=tokens_one, gates_one=gates_one, experts_one=experts_one, tokens_two=tokens_two, gates_two=gates_two, experts_two=experts_two, gate_weight=gate_weight, up_weight=up_weight, down_weight=down_weight)


def project_rows(rows, weight_block):
    return lax.dot_general(rows, weight_block, (((1,), (1,)), ((), ())), preferred_element_type=jnp.float32)


def moe_layer(tokens, gate_values, expert_ids, gate_weight, up_weight, down_weight):
    token_count = tokens.shape[0]
    flat_ids = expert_ids.reshape(-1)
    row_total = flat_ids.shape[0]
    padded_tokens = jnp.concatenate([tokens, jnp.zeros((1, tokens.shape[1]), tokens.dtype)], axis=0)
    padded_gates = jnp.concatenate([gate_values.reshape(-1), jnp.zeros((1,), jnp.float32)])
    expert_labels = jnp.arange(gate_weight.shape[0], dtype=jnp.int32)

    def per_expert(summed, inputs):
        expert_label, gate_block, up_block, down_block = inputs
        positions = jnp.nonzero(flat_ids == expert_label, size=EXPERTS * CAP, fill_value=row_total)[0].astype(jnp.int32)
        owners = jnp.where(positions < row_total, positions // TOPK, token_count).astype(jnp.int32)
        chosen = padded_tokens[owners]
        gate_sum = project_rows(chosen, gate_block)
        up_sum = project_rows(chosen, up_block)
        hidden = (jax.nn.silu(gate_sum) * up_sum).astype(jnp.bfloat16)
        result = jnp.dot(hidden, down_block, preferred_element_type=jnp.float32).astype(jnp.bfloat16)
        weights = padded_gates[positions]
        summed = summed.at[owners].add(weights[:, None] * result.astype(jnp.float32))
        return summed, None

    starting = jnp.zeros((token_count + 1, tokens.shape[1]), jnp.float32)
    summed, unused = lax.scan(per_expert, starting, (expert_labels, gate_weight, up_weight, down_weight))
    return summed[:token_count].astype(jnp.bfloat16)


def reference(tokens_one, gates_one, experts_one, tokens_two, gates_two, experts_two, gate_weight, up_weight, down_weight):
    mixed_one = moe_layer(tokens_one, gates_one, experts_one, gate_weight, up_weight, down_weight)
    mixed_two = moe_layer(tokens_two, gates_two, experts_two, gate_weight, up_weight, down_weight)
    return (mixed_one, mixed_two)
```

```python
import jax
import jax.numpy as jnp
from jax import lax
from jax.experimental import pallas as pl
from jax.experimental.pallas import tpu as pltpu
from jax.sharding import PartitionSpec as P

MESH = pl.DeviceIdType.MESH
BF16, F32 = jnp.bfloat16, jnp.float32
NT = (((1,), (1,)), ((), ()))
TN = (((0,), (0,)), ((), ()))

TOK = 24
BOTH = 2 * TOK
CAP = 6
SLOTS = 8 * CAP
ROWS = 8 * SLOTS
HID = 192
WID = 512
COPIES = 84
ALL = 8 * BOTH


def dot(a, b, dims=(((1,), (0,)), ((), ()))):
    return lax.dot_general(a, b, dims, preferred_element_type=F32)


def iota(shape, axis):
    return lax.broadcasted_iota(jnp.int32, shape, axis)


def kernel(
    tok1, gat1, exp1, tok2, gat2, exp2, gate_w, up_w, down_w,
    out1, out2,
    ZT, IG, SM, YS, SEL, WX, DW, PS, PR, PO, HT, OA, OS, OB, CM, ZF, ZS, ZR,
    ssem, rsem, lsem,
):
    e, d = lax.axis_index("expert"), lax.axis_index("dp")
    zh, x = d // 4, lax.rem(d, 4)
    zl, i8 = e // 8, lax.rem(e, 8)
    z = zh * 8 + zl
    ql = zl // 4
    q = zh * 2 + ql

    def at_z(step):
        other = lax.rem(z + step + 16, 16)
        return (lax.rem(other, 8) * 8 + i8, (other // 8) * 4 + x)

    def at_zl(step):
        return (lax.rem(zl + step + 8, 8) * 8 + i8, d)

    def at_x(step):
        return (e, zh * 4 + lax.rem(x + step + 4, 4))

    def at_yc(step):
        return (zl * 8 + lax.rem(i8 + step + 8, 8), d)

    barrier = pltpu.get_barrier_semaphore()
    greeted = (
        [at_z(k) for k in range(1, 16)]
        + [at_x(k) for k in range(1, 4)]
        + [at_yc(k) for k in range(1, 8)]
    )
    for who in greeted:
        pl.semaphore_signal(barrier, inc=1, device_id=who, device_id_type=MESH)

    copies = []

    def send(src, dst, who):
        n = len(copies)
        copy = pltpu.make_async_remote_copy(
            src_ref=src,
            dst_ref=dst,
            send_sem=ssem.at[n],
            recv_sem=rsem.at[n],
            device_id=who,
            device_id_type=MESH,
        )
        copy.start()
        copies.append(copy)
        return copy

    local = []

    def fetch(src, dst):
        copy = pltpu.make_async_copy(src, dst, lsem.at[len(local)])
        copy.start()
        local.append(copy)

    def columns(half, owner):
        return pl.ds(pl.multiple_of(half * 2048 + owner * WID, WID), WID)

    for half in range(2):
        for n, w in enumerate((gate_w, up_w)):
            fetch(
                w.at[0, :, columns(half, x)],
                WX.at[0, pl.ds(n * HID, HID), pl.ds(half * WID, WID)],
            )
    fetch(down_w.at[0], DW)

    ZT[0, q] = jnp.concatenate([tok1[...].astype(F32), tok2[...].astype(F32)], axis=0).astype(BF16)
    lane = iota((TOK, 128), 1)
    tables = []
    for gates, experts in ((gat1, exp1), (gat2, exp2)):
        table = jnp.zeros((TOK, 128), F32)
        for k in range(8):
            hit = lax.rem(lane, 64) == experts[:, k : k + 1]
            table = jnp.where(hit, gates[:, k : k + 1], table)
        high = table.astype(BF16).astype(F32)
        tables.append(jnp.where(lane < 64, high, table - high))
    IG[0, ql] = jnp.concatenate(tables, axis=0).astype(BF16)

    pl.semaphore_wait(barrier, len(greeted))

    first = [send(ZT.at[0, q], ZT.at[0, q], at_z(4 * a)) for a in (1, 2, 3)]
    first.append(send(IG.at[0, ql], IG.at[0, ql], at_z(4)))
    weights = []
    for k in (1, 3, 2):
        owner = lax.rem(x + k, 4)
        for half in range(2):
            for n, w in enumerate((gate_w, up_w)):
                weights.append(
                    send(
                        w.at[0, :, columns(half, owner)],
                        WX.at[k, pl.ds(n * HID, HID), pl.ds(half * WID, WID)],
                        at_x(k),
                    )
                )

    for copy in first:
        copy.wait_recv()
    second = []
    for b, step in ((1, -1), (3, 1), (2, 2)):
        second.append(send(IG.at[0], IG.at[b], at_z(step)))
        second.append(send(ZT.at[0], ZT.at[b], at_z(step)))

    rows, cols = iota((ALL, ALL), 0), iota((ALL, ALL), 1)
    block = rows // TOK == cols // TOK
    before = jnp.where(block & (rows < cols), 1.0, 0.0).astype(BF16)
    after = jnp.where(block & (cols < rows), 1.0, 0.0).astype(BF16)
    pick, lane = iota((128, 128), 0), iota((128, 128), 1)
    wanted = zl * 8 + lax.rem(i8 + pick, 8)
    picks = jnp.where(
        ((pick < 8) & (lane == wanted)) | ((pick >= 8) & (pick < 16) & (lane == wanted + 64)),
        1.0,
        0.0,
    ).astype(BF16)

    for copy in second:
        copy.wait_recv()

    info = IG[...].reshape(ALL, 128)
    chosen = dot(picks[:16], info, NT)
    taken = chosen > 0.0
    place = dot(jnp.where(taken, 1.0, 0.0).astype(BF16), before)
    token = iota((16, ALL), 1)
    slot = place.astype(jnp.int32) + token // BOTH * CAP
    step_of = lax.rem(token, BOTH) // TOK
    for s in range(2):
        aim = jnp.where(taken & (step_of == s), slot, -1)
        for k in range(8):
            SM[s, k * SLOTS : (k + 1) * SLOTS] = jnp.where(
                iota((SLOTS, ALL), 0) == aim[k : k + 1], 1.0, 0.0
            ).astype(BF16)
    dispatch = []
    for s in range(2):
        for half in range(2):
            held = jnp.concatenate(
                [ZT[b, 2 * half : 2 * half + 2].reshape(2 * BOTH, WID) for b in range(4)], axis=0
            )
            YS[s, :, half * WID : (half + 1) * WID] = dot(SM[s], held).astype(BF16)
        dispatch.append(
            [
                send(YS.at[s, pl.ds(k * SLOTS, SLOTS)], SEL.at[s, pl.ds(k * SLOTS, SLOTS)], at_yc(k))
                for k in range(1, 8)
            ]
        )
        SEL[s, 0:SLOTS] = YS[s, 0:SLOTS]

    gates = dot(info, picks, NT)
    count = dot(after, jnp.where(gates > 0.0, 1.0, 0.0).astype(BF16))
    base = (iota((ALL, 128), 0) // BOTH * CAP + iota((ALL, 128), 1) * SLOTS).astype(F32)
    target = jnp.where(gates > 0.0, count + base, -1.0)
    column = iota((8 * TOK, ROWS), 1).astype(F32)
    for s in range(2):
        part = lambda v: v.reshape(8, BOTH, 128)[:, s * TOK : (s + 1) * TOK].reshape(8 * TOK, 128)
        aim, value = part(target), part(gates)
        for n in range(2):
            total = jnp.zeros((8 * TOK, ROWS), F32)
            for k in range(8):
                hit = column == aim[:, k : k + 1]
                total = jnp.where(hit, value[:, 8 * n + k : 8 * n + k + 1], total)
            CM[s, n] = total.astype(BF16)

    for copy in local:
        copy.wait()
    partial = []
    for s in range(2):
        for copy in dispatch[s]:
            copy.wait_recv()
        sent = []
        for n, k in enumerate((1, 3, 2)):
            if s == 0:
                for copy in weights[4 * n : 4 * n + 4]:
                    copy.wait_recv()
            PS[s, k] = dot(WX[k], SEL[s], NT).astype(BF16)
            sent.append(send(PS.at[s, k], PR.at[s, k], at_x(-k)))
        PO[s] = dot(WX[0], SEL[s], NT)
        partial.append(sent)

    crossed, around, forwarded = [], [], []
    for s in range(2):
        for copy in partial[s]:
            copy.wait_recv()
        both = PO[s]
        for k in range(1, 4):
            both = both + PR[s, k].astype(F32)
        gate, up = both[:HID], both[HID:]
        HT[s, d] = (gate / (1.0 + jnp.exp(-gate)) * up).astype(BF16)
        crossed.append(send(HT.at[s, d], HT.at[s, d], at_z(8)))
        around.append([send(HT.at[s, d], HT.at[s, d], at_x(k)) for k in (1, 3, 2)])

    other = lax.rem(d + 4, 8)

    def pass_on(s):
        crossed[s].wait_recv()
        forwarded.append([send(HT.at[s, other], HT.at[s, other], at_x(k)) for k in (1, 3, 2)])

    returned = []

    def project(s):
        for copy in around[s] + forwarded[s]:
            copy.wait_recv()
        OA[...] = jnp.zeros((ROWS, WID), F32)

        @pl.loop(0, 8)
        def _(n):
            w = DW[pl.ds(pl.multiple_of(n * HID, HID), HID), :]
            OA[...] += dot(HT[s, n], w, TN)

        OS[s] = OA[...].astype(BF16)
        returned.append(
            [
                send(OS.at[s, pl.ds(k * SLOTS, SLOTS)], OB.at[s, pl.ds(k * SLOTS, SLOTS)], at_yc(-k))
                for k in range(1, 8)
            ]
        )
        OB[s, 0:SLOTS] = OS[s, 0:SLOTS]

    last = []

    def combine(s):
        for copy in returned[s]:
            copy.wait_recv()
        rows_in = OB[s]
        total = (dot(CM[s, 0], rows_in) + dot(CM[s, 1], rows_in)).reshape(8, TOK, WID)
        for n in range(4):
            ZF[s, :, n * TOK : (n + 1) * TOK] = total[:, :, n * 128 : (n + 1) * 128]
        ZS[s] = ZF[s].astype(BF16)
        sent = []
        for k in range(1, 8):
            block = k % 4 * 2 + lax.rem(zl + k, 8) // 4
            sent.append(send(ZS.at[s, block], ZR.at[s, k], at_zl(k)))
        last.append(sent)

    def finish(s, out):
        for copy in last[s]:
            copy.wait_recv()
        total = ZF[s, ql]
        for k in range(1, 8):
            total = total + ZR[s, k].astype(F32)
        for n in range(4):
            out[:, n * 128 : (n + 1) * 128] = total[n * TOK : (n + 1) * TOK].astype(BF16)

    pass_on(0)
    project(0)
    pass_on(1)
    combine(0)
    project(1)
    combine(1)
    finish(0, out1)
    finish(1, out2)
    for copy in copies:
        copy.wait_send()


def body(tok1, gat1, exp1, tok2, gat2, exp2, gate_w, up_w, down_w):
    vmem = pl.BlockSpec(memory_space=pltpu.VMEM)
    hbm = pl.BlockSpec(memory_space=pl.ANY)
    scratch = [
        pltpu.VMEM((4, 4, BOTH, WID), BF16),
        pltpu.VMEM((4, 2, BOTH, 128), BF16),
        pltpu.VMEM((2, ROWS, ALL), BF16),
        pltpu.VMEM((2, ROWS, 2 * WID), BF16),
        pltpu.VMEM((2, ROWS, 2 * WID), BF16),
        pltpu.VMEM((4, 2 * HID, 2 * WID), BF16),
        pltpu.VMEM((8 * HID, WID), BF16),
        pltpu.VMEM((2, 4, 2 * HID, ROWS), BF16),
        pltpu.VMEM((2, 4, 2 * HID, ROWS), BF16),
        pltpu.VMEM((2, 2 * HID, ROWS), F32),
        pltpu.VMEM((2, 8, HID, ROWS), BF16),
        pltpu.VMEM((ROWS, WID), F32),
        pltpu.VMEM((2, ROWS, WID), BF16),
        pltpu.VMEM((2, ROWS, WID), BF16),
        pltpu.VMEM((2, 2, 8 * TOK, ROWS), BF16),
        pltpu.VMEM((2, 8, 4 * TOK, 128), F32),
        pltpu.VMEM((2, 8, 4 * TOK, 128), BF16),
        pltpu.VMEM((2, 8, 4 * TOK, 128), BF16),
        pltpu.SemaphoreType.DMA((COPIES,)),
        pltpu.SemaphoreType.DMA((COPIES,)),
        pltpu.SemaphoreType.DMA((5,)),
    ]
    result = jax.ShapeDtypeStruct((TOK, WID), BF16)
    return pl.pallas_call(
        kernel,
        out_shape=(result, result),
        in_specs=[vmem] * 6 + [hbm] * 3,
        out_specs=(vmem, vmem),
        scratch_shapes=scratch,
        compiler_params=pltpu.CompilerParams(
            collective_id=0, has_side_effects=True, vmem_limit_bytes=48 * 2**20
        ),
        cost_estimate=pl.CostEstimate(
            flops=2 * 2 * ROWS * (2 * HID * 4096 + 1536 * WID),
            bytes_accessed=3 * HID * 4096 * 2,
            transcendentals=2 * HID * ROWS,
        ),
        name="moe",
    )(tok1, gat1, exp1, tok2, gat2, exp2, gate_w, up_w, down_w)


def solution(mesh):
    return jax.shard_map(
        body,
        mesh=mesh,
        in_specs=(
            P("expert", "dp"),
            P("expert", None),
            P("expert", None),
            P("expert", "dp"),
            P("expert", None),
            P("expert", None),
            P("expert", "dp", None),
            P("expert", "dp", None),
            P("expert", None, "dp"),
        ),
        out_specs=(P("expert", "dp"), P("expert", "dp")),
        check_vma=False,
    )
```

```python
import jax
import jax.numpy as jnp
from jax import lax
from jax.experimental import pallas as pl
from jax.experimental.pallas import tpu as pltpu
from jax.sharding import PartitionSpec as P

MESH = pl.DeviceIdType.MESH
BF16, F32 = jnp.bfloat16, jnp.float32
NT = (((1,), (1,)), ((), ()))
TN = (((0,), (0,)), ((), ()))

TOK = 24
BOTH = 2 * TOK
CAP = 6
SLOTS = 8 * CAP
ROWS = 8 * SLOTS
HID = 192
WID = 512
COPIES = 127
HEAD = 32
CHUNKS = (((0, 384),), ((0, 256), (256, 384)))
AROUND = ((1, -1), (3, 1), (2, 2))
ALL = 8 * BOTH


def dot(a, b, dims=(((1,), (0,)), ((), ()))):
    return lax.dot_general(a, b, dims, preferred_element_type=F32)


def iota(shape, axis):
    return lax.broadcasted_iota(jnp.int32, shape, axis)


def kernel(
    tok1, gat1, exp1, tok2, gat2, exp2, gate_w, up_w, down_w,
    out1, out2,
    TV, GV, EV, ZT, IG, SM, YS, TK, WO, WA, WB, DW, PS, PR, PO, HT, OA, OS, OB, CM, ZF, ZS, ZR,
    ssem, rsem, lsem,
):
    e, d = lax.axis_index("expert"), lax.axis_index("dp")
    zh, x = d // 4, lax.rem(d, 4)
    zl, i8 = e // 8, lax.rem(e, 8)
    z = zh * 8 + zl
    ql = zl // 4
    q = zh * 2 + ql
    xa, xb, xc = x + 1 - 2 * lax.rem(x, 2), 3 - x, lax.rem(x + 2, 4)

    def at_z(step):
        other = lax.rem(z + step + 16, 16)
        return (lax.rem(other, 8) * 8 + i8, (other // 8) * 4 + x)

    def at_zl(step):
        return (lax.rem(zl + step + 8, 8) * 8 + i8, d)

    def at_x(place):
        return (e, zh * 4 + place)

    def at_yc(step):
        return (zl * 8 + lax.rem(i8 + step + 8, 8), d)

    barrier = pltpu.get_barrier_semaphore()
    greeted = (
        [at_z(k) for k in range(1, 16)]
        + [at_x(place) for place in (xa, xb, xc)]
        + [at_yc(k) for k in range(1, 8)]
    )
    for who in greeted:
        pl.semaphore_signal(barrier, inc=1, device_id=who, device_id_type=MESH)

    local = []

    def fetch(src, dst):
        copy = pltpu.make_async_copy(src, dst, lsem.at[len(local)])
        copy.start()
        local.append(copy)

    def columns(half, owner):
        return pl.ds(pl.multiple_of(half * 2048 + owner * WID, WID), WID)

    for n, (tok, gat, exp) in enumerate(((tok1, gat1, exp1), (tok2, gat2, exp2))):
        fetch(tok, TV.at[n])
        fetch(gat, GV.at[n])
        fetch(exp, EV.at[n])
    for m, cols in enumerate((columns(0, xa), columns(0, x), columns(1, x), columns(1, xb))):
        for n, w in enumerate((gate_w, up_w)):
            fetch(w.at[0, :, cols], WO.at[pl.ds(n * HID, HID), pl.ds(m * WID, WID)])
    fetch(down_w.at[0], DW)

    copies = []

    def send(src, dst, who):
        n = len(copies)
        copy = pltpu.make_async_remote_copy(
            src_ref=src,
            dst_ref=dst,
            send_sem=ssem.at[n],
            recv_sem=rsem.at[n],
            device_id=who,
            device_id_type=MESH,
        )
        copy.start()
        copies.append(copy)
        return copy

    for copy in local[:6]:
        copy.wait()
    ZT[0, q] = jnp.concatenate([TV[0].astype(F32), TV[1].astype(F32)], axis=0).astype(BF16)
    label = iota((128, TOK), 0)
    unit = jnp.where(iota((128, 128), 0) == iota((128, 128), 1), 1.0, 0.0).astype(BF16)
    tables = []
    for s in range(2):
        gates, experts = GV[s], EV[s]
        table = jnp.zeros((128, TOK), F32)
        for k in range(8):
            hit = lax.rem(label, 64) == experts[k : k + 1]
            table = jnp.where(hit, gates[k : k + 1], table)
        high = table.astype(BF16).astype(F32)
        tables.append(dot(jnp.where(label < 64, high, table - high).astype(BF16), unit, TN))
    IG[0, ql] = jnp.concatenate(tables, axis=0).astype(BF16)

    pl.semaphore_wait(barrier, len(greeted))

    parts = (pl.ds(0, HEAD), pl.ds(HEAD, BOTH - HEAD))
    first, second, table_second = {}, ([], []), []

    def spread(n, a):
        block = lax.rem(q - a + 4, 4)
        for b, step in AROUND:
            src = ZT.at[0, block, parts[n]]
            second[n].append(send(src, ZT.at[b, block, parts[n]], at_z(step)))

    table_first = send(IG.at[0, ql], IG.at[0, ql], at_z(4))
    for a in (2, 1, 3):
        first[0, a] = send(ZT.at[0, q, parts[0]], ZT.at[0, q, parts[0]], at_z(4 * a))
    spread(0, 0)
    table_first.wait_recv()
    table_second += [send(IG.at[0], IG.at[b], at_z(step)) for b, step in AROUND]
    for a in (1, 3):
        first[0, a].wait_recv()
        spread(0, a)
    for a in (2, 1, 3):
        first[1, a] = send(ZT.at[0, q, parts[1]], ZT.at[0, q, parts[1]], at_z(4 * a))
    first[0, 2].wait_recv()
    spread(0, 2)
    spread(1, 0)
    weights = []
    for cols, buffer, place in (
        ((columns(1, xa), columns(1, xc)), WA, xa),
        ((columns(0, xc), columns(0, xb)), WB, xb),
    ):
        for m in range(2):
            for h, w in enumerate((gate_w, up_w)):
                dst = buffer.at[pl.ds(h * HID, HID), pl.ds(m * WID, WID)]
                weights.append(send(w.at[0, :, cols[m]], dst, at_x(place)))
    for a in (1, 3, 2):
        first[1, a].wait_recv()
        spread(1, a)

    rows, cols = iota((ALL, ALL), 0), iota((ALL, ALL), 1)
    block = rows // TOK == cols // TOK
    before = jnp.where(block & (rows < cols), 1.0, 0.0).astype(BF16)
    after = jnp.where(block & (cols < rows), 1.0, 0.0).astype(BF16)
    pick, lane = iota((128, 128), 0), iota((128, 128), 1)
    wanted = zl * 8 + lax.rem(i8 + pick, 8)
    picks = jnp.where(
        ((pick < 8) & (lane == wanted)) | ((pick >= 8) & (pick < 16) & (lane == wanted + 64)),
        1.0,
        0.0,
    ).astype(BF16)

    for copy in table_second:
        copy.wait_recv()
    info = IG[...].reshape(ALL, 128)
    chosen = dot(picks[:16], info, NT)
    taken = chosen > 0.0
    place = dot(jnp.where(taken, 1.0, 0.0).astype(BF16), before)
    token = iota((16, ALL), 1)
    slot = place.astype(jnp.int32) + token // BOTH * CAP
    step_of = lax.rem(token, BOTH) // TOK
    held_row, all_row = iota((8 * HEAD, ALL), 0), iota((8 * HEAD, ALL), 1)
    for s in range(2):
        aim = jnp.where(taken & (step_of == s), slot, -1).astype(F32)
        same = held_row // HEAD * BOTH + lax.rem(held_row, HEAD) + s * (BOTH - HEAD) == all_row
        aim = dot(aim.astype(BF16), jnp.where(same, 1.0, 0.0).astype(BF16), NT)
        for k in range(8):
            SM[s, k * SLOTS : (k + 1) * SLOTS] = jnp.where(
                iota((SLOTS, 8 * HEAD), 0).astype(F32) == aim[k : k + 1], 1.0, 0.0
            ).astype(BF16)
    dispatch = []

    def select(s):
        start = s * (BOTH - HEAD)
        for half in range(2):
            held = ZT[:, 2 * half : 2 * half + 2, start : start + HEAD].reshape(8 * HEAD, WID)
            YS[s, :, half * WID : (half + 1) * WID] = dot(SM[s], held).astype(BF16)
        TK[s, 0:SLOTS, WID : 3 * WID] = YS[s, 0:SLOTS]

    def deliver(s):
        sent = []
        for k in range(1, 8):
            group = pl.ds(k * SLOTS, SLOTS)
            sent.append(send(YS.at[s, group], TK.at[s, group, pl.ds(WID, 2 * WID)], at_yc(k)))
        dispatch.append(sent)

    for copy in second[0]:
        copy.wait_recv()
    select(0)
    deliver(0)

    gates = dot(info, picks, NT)
    count = dot(after, jnp.where(gates > 0.0, 1.0, 0.0).astype(BF16))
    base = (iota((ALL, 128), 0) // BOTH * CAP + iota((ALL, 128), 1) * SLOTS).astype(F32)
    target = jnp.where(gates > 0.0, count + base, -1.0)
    column = iota((8 * TOK, ROWS), 1).astype(F32)
    for s in range(2):
        part = lambda v: v.reshape(8, BOTH, 128)[:, s * TOK : (s + 1) * TOK].reshape(8 * TOK, 128)
        aim, value = part(target), part(gates)
        for n in range(2):
            total = jnp.zeros((8 * TOK, ROWS), F32)
            for k in range(8):
                hit = column == aim[:, k : k + 1]
                total = jnp.where(hit, value[:, 8 * n + k : 8 * n + k + 1], total)
            CM[s, n] = total.astype(BF16)

    for copy in second[1]:
        copy.wait_recv()
    select(1)

    shared = []

    def share(s):
        sent = []
        for group in range(4):
            for k in (2 * group, 2 * group + 1):
                if k > 0:
                    dispatch[s][k - 1].wait_recv()
            rows = pl.ds(2 * group * SLOTS, 2 * SLOTS)
            for m, to, who in ((1, 0, xa), (2, 3, xb)):
                src = TK.at[s, rows, pl.ds(m * WID, WID)]
                sent.append(send(src, TK.at[s, rows, pl.ds(to * WID, WID)], at_x(who)))
        shared.append(sent)

    partial, crossed, around, passed = {}, {}, {}, {}
    other = lax.rem(d + 4, 8)

    def sums(s):
        for copy in shared[s]:
            copy.wait_recv()
        if s == 0:
            for copy in weights:
                copy.wait_recv()
        for c in CHUNKS[s]:
            partial[s, c] = []
            lanes = pl.ds(c[0], c[1] - c[0])
            for n, (w, start, who) in enumerate(((WA, 2 * WID, xa), (WB, 0, xb))):
                rows = TK[s, c[0] : c[1], start : start + 2 * WID]
                PS[s, n, :, c[0] : c[1]] = dot(w[...], rows, NT).astype(BF16)
                partial[s, c].append(send(PS.at[s, n, :, lanes], PR.at[s, n, :, lanes], at_x(who)))
        if s == 0:
            for copy in local[6:]:
                copy.wait()
        PO[s] = dot(WO[...], TK[s], NT)

    def held(s, c, block):
        return HT.at[s, block, :, pl.ds(c[0], c[1] - c[0])]

    def move(s, c, block, who):
        return send(held(s, c, block), held(s, c, block), who)

    def hidden(s, c):
        for copy in partial[s, c]:
            copy.wait_recv()
        both = PO[s, :, c[0] : c[1]]
        for n in range(2):
            both = both + PR[s, n, :, c[0] : c[1]].astype(F32)
        gate, up = both[:HID], both[HID:]
        HT[s, d, :, c[0] : c[1]] = (gate / (1.0 + jnp.exp(-gate)) * up).astype(BF16)
        crossed[s, c] = move(s, c, d, at_z(8))

    def go_round(s, c):
        around[s, c] = [move(s, c, d, at_x(place)) for place in (xa, xb)]

    def relay(s, c):
        around[s, c][0].wait_recv()
        around[s, c].append(move(s, c, zh * 4 + xa, at_x(xb)))

    def pass_on(s, c):
        crossed[s, c].wait_recv()
        passed[s, c] = [move(s, c, other, at_x(place)) for place in (xa, xb)]

    def pass_relay(s, c):
        passed[s, c][1].wait_recv()
        passed[s, c].append(move(s, c, 4 - zh * 4 + xb, at_x(xa)))

    def add(s, c, start):
        @pl.loop(0, 4)
        def _(n):
            w = DW[pl.ds(pl.multiple_of((start + n) * HID, HID), HID), :]
            OA[s, c[0] : c[1]] += dot(HT[s, start + n, :, c[0] : c[1]], w, TN)

    def project_own(s, c):
        for copy in around[s, c][1:]:
            copy.wait_recv()
        OA[s, c[0] : c[1]] = jnp.zeros((c[1] - c[0], WID), F32)
        add(s, c, zh * 4)

    returned = ([], [])

    def project(s, c):
        for copy in (passed[s, c][0], passed[s, c][2]):
            copy.wait_recv()
        add(s, c, 4 - zh * 4)
        OS[s, c[0] : c[1]] = OA[s, c[0] : c[1]].astype(BF16)
        for k in range(c[0] // SLOTS, c[1] // SLOTS):
            group = pl.ds(k * SLOTS, SLOTS)
            if k == 0:
                OB[s, 0:SLOTS] = OS[s, 0:SLOTS]
            else:
                returned[s].append(send(OS.at[s, group], OB.at[s, group], at_yc(-k)))

    last = []

    def combine(s):
        for copy in returned[s]:
            copy.wait_recv()
        rows_in = OB[s]
        total = (dot(CM[s, 0], rows_in) + dot(CM[s, 1], rows_in)).reshape(8, TOK, WID)
        for n in range(4):
            ZF[s, :, n * TOK : (n + 1) * TOK] = total[:, :, n * 128 : (n + 1) * 128]
        ZS[s] = ZF[s].astype(BF16)
        sent = []
        for k in range(1, 8):
            block = k % 4 * 2 + lax.rem(zl + k, 8) // 4
            sent.append(send(ZS.at[s, block], ZR.at[s, k], at_zl(k)))
        last.append(sent)

    def finish(s, out):
        for copy in last[s]:
            copy.wait_recv()
        total = ZF[s, ql]
        for k in range(1, 8):
            total = total + ZR[s, k].astype(F32)
        for n in range(4):
            out[:, n * 128 : (n + 1) * 128] = total[n * TOK : (n + 1) * TOK].astype(BF16)

    (one,), (two, three) = CHUNKS
    share(0)
    deliver(1)
    sums(0)
    share(1)
    hidden(0, one)
    go_round(0, one)
    sums(1)
    relay(0, one)
    hidden(1, two)
    go_round(1, two)
    hidden(1, three)
    go_round(1, three)
    pass_on(0, one)
    project_own(0, one)
    relay(1, two)
    relay(1, three)
    pass_relay(0, one)
    pass_on(1, two)
    project(0, one)
    pass_on(1, three)
    pass_relay(1, two)
    project_own(1, two)
    project_own(1, three)
    pass_relay(1, three)
    project(1, two)
    combine(0)
    project(1, three)
    combine(1)
    finish(0, out1)
    finish(1, out2)
    for copy in copies:
        copy.wait_send()
    assert len(copies) == COPIES


def body(tok1, gat1, exp1, tok2, gat2, exp2, gate_w, up_w, down_w):
    vmem = pl.BlockSpec(memory_space=pltpu.VMEM)
    hbm = pl.BlockSpec(memory_space=pl.ANY)
    scratch = [
        pltpu.VMEM((2, TOK, WID), BF16),
        pltpu.VMEM((2, 8, TOK), F32),
        pltpu.VMEM((2, 8, TOK), jnp.int32),
        pltpu.VMEM((4, 4, BOTH, WID), BF16),
        pltpu.VMEM((4, 2, BOTH, 128), BF16),
        pltpu.VMEM((2, ROWS, 8 * HEAD), BF16),
        pltpu.VMEM((2, ROWS, 2 * WID), BF16),
        pltpu.VMEM((2, ROWS, 4 * WID), BF16),
        pltpu.VMEM((2 * HID, 4 * WID), BF16),
        pltpu.VMEM((2 * HID, 2 * WID), BF16),
        pltpu.VMEM((2 * HID, 2 * WID), BF16),
        pltpu.VMEM((8 * HID, WID), BF16),
        pltpu.VMEM((2, 2, 2 * HID, ROWS), BF16),
        pltpu.VMEM((2, 2, 2 * HID, ROWS), BF16),
        pltpu.VMEM((2, 2 * HID, ROWS), F32),
        pltpu.VMEM((2, 8, HID, ROWS), BF16),
        pltpu.VMEM((2, ROWS, WID), F32),
        pltpu.VMEM((2, ROWS, WID), BF16),
        pltpu.VMEM((2, ROWS, WID), BF16),
        pltpu.VMEM((2, 2, 8 * TOK, ROWS), BF16),
        pltpu.VMEM((2, 8, 4 * TOK, 128), F32),
        pltpu.VMEM((2, 8, 4 * TOK, 128), BF16),
        pltpu.VMEM((2, 8, 4 * TOK, 128), BF16),
        pltpu.SemaphoreType.DMA((COPIES,)),
        pltpu.SemaphoreType.DMA((COPIES,)),
        pltpu.SemaphoreType.DMA((15,)),
    ]
    result = jax.ShapeDtypeStruct((TOK, WID), BF16)
    return pl.pallas_call(
        kernel,
        out_shape=(result, result),
        in_specs=[hbm] * 9,
        out_specs=(vmem, vmem),
        scratch_shapes=scratch,
        compiler_params=pltpu.CompilerParams(
            collective_id=0, has_side_effects=True, vmem_limit_bytes=60 * 2**20
        ),
        cost_estimate=pl.CostEstimate(
            flops=2 * 2 * ROWS * (2 * HID * 4096 + 1536 * WID),
            bytes_accessed=3 * HID * 4096 * 2,
            transcendentals=2 * HID * ROWS,
        ),
        name="moe",
    )(tok1, gat1.T, exp1.T, tok2, gat2.T, exp2.T, gate_w, up_w, down_w)


def solution(mesh):
    return jax.shard_map(
        body,
        mesh=mesh,
        in_specs=(
            P("expert", "dp"),
            P("expert", None),
            P("expert", None),
            P("expert", "dp"),
            P("expert", None),
            P("expert", None),
            P("expert", "dp", None),
            P("expert", "dp", None),
            P("expert", None, "dp"),
        ),
        out_specs=(P("expert", "dp"), P("expert", "dp")),
        check_vma=False,
    )
```

```python
import jax
import jax.numpy as jnp
from jax import lax
from jax.experimental import pallas as pl
from jax.experimental.pallas import tpu as pltpu
from jax.sharding import PartitionSpec as P

MESH = pl.DeviceIdType.MESH
BF16, F32 = jnp.bfloat16, jnp.float32
NT = (((1,), (1,)), ((), ()))
TN = (((0,), (0,)), ((), ()))

TOK = 24
BOTH = 2 * TOK
CAP = 6
SLOTS = 8 * CAP
ROWS = 8 * SLOTS
HID = 192
WID = 512
COPIES = 127
HEAD = 32
CHUNKS = (((0, 384),), ((0, 256), (256, 384)))
AROUND = ((1, -1), (3, 1), (2, 2))
ALL = 8 * BOTH


def dot(a, b, dims=(((1,), (0,)), ((), ()))):
    return lax.dot_general(a, b, dims, preferred_element_type=F32)


def iota(shape, axis):
    return lax.broadcasted_iota(jnp.int32, shape, axis)


def kernel(
    tok1, gat1, exp1, tok2, gat2, exp2, gate_w, up_w, down_w,
    out1, out2,
    TV, GV, EV, ZT, IG, SM, YS, TK, WO, WA, WB, DW, PS, PR, PO, HT, OA, OS, OB, CM, ZF, ZS, ZR,
    ssem, rsem, lsem,
):
    e, d = lax.axis_index("expert"), lax.axis_index("dp")
    zh, x = d // 4, lax.rem(d, 4)
    zl, i8 = e // 8, lax.rem(e, 8)
    z = zh * 8 + zl
    ql = zl // 4
    q = zh * 2 + ql
    xa, xb, xc = x + 1 - 2 * lax.rem(x, 2), 3 - x, lax.rem(x + 2, 4)

    def at_z(step):
        other = lax.rem(z + step + 16, 16)
        return (lax.rem(other, 8) * 8 + i8, (other // 8) * 4 + x)

    def at_zl(step):
        return (lax.rem(zl + step + 8, 8) * 8 + i8, d)

    def at_x(place):
        return (e, zh * 4 + place)

    def at_yc(step):
        return (zl * 8 + lax.rem(i8 + step + 8, 8), d)

    barrier = pltpu.get_barrier_semaphore()
    greeted = (
        [at_z(k) for k in range(1, 16)]
        + [at_x(place) for place in (xa, xb, xc)]
        + [at_yc(k) for k in range(1, 8)]
    )
    for who in greeted:
        pl.semaphore_signal(barrier, inc=1, device_id=who, device_id_type=MESH)

    local = []

    def fetch(src, dst):
        copy = pltpu.make_async_copy(src, dst, lsem.at[len(local)])
        copy.start()
        local.append(copy)

    def columns(half, owner):
        return pl.ds(pl.multiple_of(half * 2048 + owner * WID, WID), WID)

    for n, (tok, gat, exp) in enumerate(((tok1, gat1, exp1), (tok2, gat2, exp2))):
        fetch(tok, TV.at[n])
        fetch(gat, GV.at[n])
        fetch(exp, EV.at[n])
    for m, cols in enumerate((columns(0, xa), columns(0, x), columns(1, x), columns(1, xb))):
        for n, w in enumerate((gate_w, up_w)):
            fetch(w.at[0, :, cols], WO.at[pl.ds(n * HID, HID), pl.ds(m * WID, WID)])
    fetch(down_w.at[0], DW)

    copies = []

    def send(src, dst, who):
        n = len(copies)
        copy = pltpu.make_async_remote_copy(
            src_ref=src,
            dst_ref=dst,
            send_sem=ssem.at[n],
            recv_sem=rsem.at[n],
            device_id=who,
            device_id_type=MESH,
        )
        copy.start()
        copies.append(copy)
        return copy

    for copy in local[:6]:
        copy.wait()
    ZT[0, q] = jnp.concatenate([TV[0].astype(F32), TV[1].astype(F32)], axis=0).astype(BF16)
    label = iota((128, TOK), 0)
    unit = jnp.where(iota((128, 128), 0) == iota((128, 128), 1), 1.0, 0.0).astype(BF16)
    tables = []
    for s in range(2):
        gates, experts = GV[s], EV[s]
        table = jnp.zeros((128, TOK), F32)
        for k in range(8):
            hit = lax.rem(label, 64) == experts[k : k + 1]
            table = jnp.where(hit, gates[k : k + 1], table)
        high = table.astype(BF16).astype(F32)
        tables.append(dot(jnp.where(label < 64, high, table - high).astype(BF16), unit, TN))
    IG[0, ql] = jnp.concatenate(tables, axis=0).astype(BF16)

    pl.semaphore_wait(barrier, len(greeted))

    parts = (pl.ds(0, HEAD), pl.ds(HEAD, BOTH - HEAD))
    first, second, table_second = {}, ([], []), []

    def spread(n, a):
        block = lax.rem(q - a + 4, 4)
        for b, step in AROUND:
            src = ZT.at[0, block, parts[n]]
            second[n].append(send(src, ZT.at[b, block, parts[n]], at_z(step)))

    table_first = send(IG.at[0, ql], IG.at[0, ql], at_z(4))
    for a in (2, 1, 3):
        first[0, a] = send(ZT.at[0, q, parts[0]], ZT.at[0, q, parts[0]], at_z(4 * a))
    spread(0, 0)
    table_first.wait_recv()
    table_second += [send(IG.at[0], IG.at[b], at_z(step)) for b, step in AROUND]
    for a in (1, 3):
        first[0, a].wait_recv()
        spread(0, a)
    for a in (2, 1, 3):
        first[1, a] = send(ZT.at[0, q, parts[1]], ZT.at[0, q, parts[1]], at_z(4 * a))
    first[0, 2].wait_recv()
    spread(0, 2)
    spread(1, 0)
    weights = []
    for cols, buffer, place in (
        ((columns(1, xa), columns(1, xc)), WA, xa),
        ((columns(0, xc), columns(0, xb)), WB, xb),
    ):
        for m in range(2):
            for h, w in enumerate((gate_w, up_w)):
                dst = buffer.at[pl.ds(h * HID, HID), pl.ds(m * WID, WID)]
                weights.append(send(w.at[0, :, cols[m]], dst, at_x(place)))
    for a in (1, 3, 2):
        first[1, a].wait_recv()
        spread(1, a)

    rows, cols = iota((ALL, ALL), 0), iota((ALL, ALL), 1)
    block = rows // TOK == cols // TOK
    before = jnp.where(block & (rows < cols), 1.0, 0.0).astype(BF16)
    after = jnp.where(block & (cols < rows), 1.0, 0.0).astype(BF16)
    pick, lane = iota((128, 128), 0), iota((128, 128), 1)
    wanted = zl * 8 + lax.rem(i8 + pick, 8)
    picks = jnp.where(
        ((pick < 8) & (lane == wanted)) | ((pick >= 8) & (pick < 16) & (lane == wanted + 64)),
        1.0,
        0.0,
    ).astype(BF16)

    for copy in table_second:
        copy.wait_recv()
    info = IG[...].reshape(ALL, 128)
    chosen = dot(picks[:16], info, NT)
    taken = chosen > 0.0
    place = dot(jnp.where(taken, 1.0, 0.0).astype(BF16), before)
    token = iota((16, ALL), 1)
    slot = place.astype(jnp.int32) + token // BOTH * CAP
    step_of = lax.rem(token, BOTH) // TOK
    held_row, all_row = iota((8 * HEAD, ALL), 0), iota((8 * HEAD, ALL), 1)
    for s in range(2):
        aim = jnp.where(taken & (step_of == s), slot, -1).astype(F32)
        same = held_row // HEAD * BOTH + lax.rem(held_row, HEAD) + s * (BOTH - HEAD) == all_row
        aim = dot(aim.astype(BF16), jnp.where(same, 1.0, 0.0).astype(BF16), NT)
        for k in range(8):
            SM[s, k * SLOTS : (k + 1) * SLOTS] = jnp.where(
                iota((SLOTS, 8 * HEAD), 0).astype(F32) == aim[k : k + 1], 1.0, 0.0
            ).astype(BF16)
    dispatch = []

    def select(s):
        start = s * (BOTH - HEAD)
        for half in range(2):
            held = ZT[:, 2 * half : 2 * half + 2, start : start + HEAD].reshape(8 * HEAD, WID)
            YS[s, :, half * WID : (half + 1) * WID] = dot(SM[s], held).astype(BF16)
        TK[s, 0:SLOTS, WID : 3 * WID] = YS[s, 0:SLOTS]

    def deliver(s):
        sent = []
        for k in range(1, 8):
            group = pl.ds(k * SLOTS, SLOTS)
            sent.append(send(YS.at[s, group], TK.at[s, group, pl.ds(WID, 2 * WID)], at_yc(k)))
        dispatch.append(sent)

    for copy in second[0]:
        copy.wait_recv()
    select(0)
    deliver(0)

    gates = dot(info, picks, NT)
    count = dot(after, jnp.where(gates > 0.0, 1.0, 0.0).astype(BF16))
    base = (iota((ALL, 128), 0) // BOTH * CAP + iota((ALL, 128), 1) * SLOTS).astype(F32)
    target = jnp.where(gates > 0.0, count + base, -1.0)
    column = iota((8 * TOK, ROWS), 1).astype(F32)
    for s in range(2):
        part = lambda v: v.reshape(8, BOTH, 128)[:, s * TOK : (s + 1) * TOK].reshape(8 * TOK, 128)
        aim, value = part(target), part(gates)
        for n in range(2):
            total = jnp.zeros((8 * TOK, ROWS), F32)
            for k in range(8):
                hit = column == aim[:, k : k + 1]
                total = jnp.where(hit, value[:, 8 * n + k : 8 * n + k + 1], total)
            CM[s, n] = total.astype(BF16)

    for copy in second[1]:
        copy.wait_recv()
    select(1)

    shared = []

    def share(s):
        sent = []
        for group in range(4):
            for k in (2 * group, 2 * group + 1):
                if k > 0:
                    dispatch[s][k - 1].wait_recv()
            rows = pl.ds(2 * group * SLOTS, 2 * SLOTS)
            for m, to, who in ((1, 0, xa), (2, 3, xb)):
                src = TK.at[s, rows, pl.ds(m * WID, WID)]
                sent.append(send(src, TK.at[s, rows, pl.ds(to * WID, WID)], at_x(who)))
        shared.append(sent)

    partial, crossed, around, passed = {}, {}, {}, {}
    other = lax.rem(d + 4, 8)

    def sums(s):
        for copy in shared[s]:
            copy.wait_recv()
        if s == 0:
            for copy in weights:
                copy.wait_recv()
        for c in CHUNKS[s]:
            partial[s, c] = []
            lanes = pl.ds(c[0], c[1] - c[0])
            for n, (w, start, who) in enumerate(((WA, 2 * WID, xa), (WB, 0, xb))):
                rows = TK[s, c[0] : c[1], start : start + 2 * WID]
                PS[s, n, :, c[0] : c[1]] = dot(w[...], rows, NT).astype(BF16)
                partial[s, c].append(send(PS.at[s, n, :, lanes], PR.at[s, n, :, lanes], at_x(who)))
        if s == 0:
            for copy in local[6:]:
                copy.wait()
        PO[s] = dot(WO[...], TK[s], NT)

    def held(s, c, block):
        return HT.at[s, block, :, pl.ds(c[0], c[1] - c[0])]

    def move(s, c, block, who):
        return send(held(s, c, block), held(s, c, block), who)

    def hidden(s, c):
        for copy in partial[s, c]:
            copy.wait_recv()
        both = PO[s, :, c[0] : c[1]]
        for n in range(2):
            both = both + PR[s, n, :, c[0] : c[1]].astype(F32)
        gate, up = both[:HID], both[HID:]
        HT[s, d, :, c[0] : c[1]] = (gate / (1.0 + jnp.exp(-gate)) * up).astype(BF16)
        crossed[s, c] = move(s, c, d, at_z(8))

    def go_round(s, c):
        around[s, c] = [move(s, c, d, at_x(place)) for place in ((xa, xb, xc) if c[1] - c[0] == 128 else (xa, xb))]

    def relay(s, c):
        around[s, c][0].wait_recv()
        around[s, c].append(move(s, c, zh * 4 + xa, at_x(xb)))

    def pass_on(s, c):
        crossed[s, c].wait_recv()
        places = (xa, xb, xc) if c[1] - c[0] == 128 else (xa, xb)
        passed[s, c] = [move(s, c, other, at_x(place)) for place in places]

    def pass_relay(s, c):
        passed[s, c][1].wait_recv()
        passed[s, c].append(move(s, c, 4 - zh * 4 + xb, at_x(xa)))

    def add(s, c, start):
        @pl.loop(0, 4)
        def _(n):
            w = DW[pl.ds(pl.multiple_of((start + n) * HID, HID), HID), :]
            OA[s, c[0] : c[1]] += dot(HT[s, start + n, :, c[0] : c[1]], w, TN)

    def project_own(s, c):
        for copy in around[s, c][0 if c[1] - c[0] == 128 else 1 :]:
            copy.wait_recv()
        OA[s, c[0] : c[1]] = jnp.zeros((c[1] - c[0], WID), F32)
        add(s, c, zh * 4)

    returned = ([], [])

    def project(s, c):
        for n in (0, 1, 2) if c[1] - c[0] == 128 else (0, 2):
            passed[s, c][n].wait_recv()
        add(s, c, 4 - zh * 4)
        OS[s, c[0] : c[1]] = OA[s, c[0] : c[1]].astype(BF16)
        for k in range(c[0] // SLOTS, c[1] // SLOTS):
            group = pl.ds(k * SLOTS, SLOTS)
            if k == 0:
                OB[s, 0:SLOTS] = OS[s, 0:SLOTS]
            else:
                returned[s].append(send(OS.at[s, group], OB.at[s, group], at_yc(-k)))

    last = []

    def combine(s):
        for copy in returned[s]:
            copy.wait_recv()
        rows_in = OB[s]
        total = (dot(CM[s, 0], rows_in) + dot(CM[s, 1], rows_in)).reshape(8, TOK, WID)
        for n in range(4):
            ZF[s, :, n * TOK : (n + 1) * TOK] = total[:, :, n * 128 : (n + 1) * 128]
        ZS[s] = ZF[s].astype(BF16)
        sent = []
        for k in range(1, 8):
            block = k % 4 * 2 + lax.rem(zl + k, 8) // 4
            sent.append(send(ZS.at[s, block], ZR.at[s, k], at_zl(k)))
        last.append(sent)

    def finish(s, out):
        for copy in last[s]:
            copy.wait_recv()
        total = ZF[s, ql]
        for k in range(1, 8):
            total = total + ZR[s, k].astype(F32)
        for n in range(4):
            out[:, n * 128 : (n + 1) * 128] = total[n * TOK : (n + 1) * TOK].astype(BF16)

    (one,), (two, three) = CHUNKS
    share(0)
    deliver(1)
    sums(0)
    share(1)
    hidden(0, one)
    go_round(0, one)
    sums(1)
    relay(0, one)
    hidden(1, two)
    go_round(1, two)
    hidden(1, three)
    go_round(1, three)
    pass_on(0, one)
    project_own(0, one)
    relay(1, two)
    pass_relay(0, one)
    pass_on(1, two)
    project(0, one)
    pass_on(1, three)
    pass_relay(1, two)
    project_own(1, two)
    project_own(1, three)
    project(1, two)
    combine(0)
    project(1, three)
    combine(1)
    finish(0, out1)
    finish(1, out2)
    for copy in copies:
        copy.wait_send()
    assert len(copies) == COPIES


def body(tok1, gat1, exp1, tok2, gat2, exp2, gate_w, up_w, down_w):
    vmem = pl.BlockSpec(memory_space=pltpu.VMEM)
    hbm = pl.BlockSpec(memory_space=pl.ANY)
    scratch = [
        pltpu.VMEM((2, TOK, WID), BF16),
        pltpu.VMEM((2, 8, TOK), F32),
        pltpu.VMEM((2, 8, TOK), jnp.int32),
        pltpu.VMEM((4, 4, BOTH, WID), BF16),
        pltpu.VMEM((4, 2, BOTH, 128), BF16),
        pltpu.VMEM((2, ROWS, 8 * HEAD), BF16),
        pltpu.VMEM((2, ROWS, 2 * WID), BF16),
        pltpu.VMEM((2, ROWS, 4 * WID), BF16),
        pltpu.VMEM((2 * HID, 4 * WID), BF16),
        pltpu.VMEM((2 * HID, 2 * WID), BF16),
        pltpu.VMEM((2 * HID, 2 * WID), BF16),
        pltpu.VMEM((8 * HID, WID), BF16),
        pltpu.VMEM((2, 2, 2 * HID, ROWS), BF16),
        pltpu.VMEM((2, 2, 2 * HID, ROWS), BF16),
        pltpu.VMEM((2, 2 * HID, ROWS), F32),
        pltpu.VMEM((2, 8, HID, ROWS), BF16),
        pltpu.VMEM((2, ROWS, WID), F32),
        pltpu.VMEM((2, ROWS, WID), BF16),
        pltpu.VMEM((2, ROWS, WID), BF16),
        pltpu.VMEM((2, 2, 8 * TOK, ROWS), BF16),
        pltpu.VMEM((2, 8, 4 * TOK, 128), F32),
        pltpu.VMEM((2, 8, 4 * TOK, 128), BF16),
        pltpu.VMEM((2, 8, 4 * TOK, 128), BF16),
        pltpu.SemaphoreType.DMA((COPIES,)),
        pltpu.SemaphoreType.DMA((COPIES,)),
        pltpu.SemaphoreType.DMA((15,)),
    ]
    result = jax.ShapeDtypeStruct((TOK, WID), BF16)
    return pl.pallas_call(
        kernel,
        out_shape=(result, result),
        in_specs=[hbm] * 9,
        out_specs=(vmem, vmem),
        scratch_shapes=scratch,
        compiler_params=pltpu.CompilerParams(
            collective_id=0, has_side_effects=True, vmem_limit_bytes=60 * 2**20
        ),
        cost_estimate=pl.CostEstimate(
            flops=2 * 2 * ROWS * (2 * HID * 4096 + 1536 * WID),
            bytes_accessed=3 * HID * 4096 * 2,
            transcendentals=2 * HID * ROWS,
        ),
        name="moe",
    )(tok1, gat1.T, exp1.T, tok2, gat2.T, exp2.T, gate_w, up_w, down_w)


def solution(mesh):
    return jax.shard_map(
        body,
        mesh=mesh,
        in_specs=(
            P("expert", "dp"),
            P("expert", None),
            P("expert", None),
            P("expert", "dp"),
            P("expert", None),
            P("expert", None),
            P("expert", "dp", None),
            P("expert", "dp", None),
            P("expert", None, "dp"),
        ),
        out_specs=(P("expert", "dp"), P("expert", "dp")),
        check_vma=False,
    )
```

```python
import jax
import jax.numpy as jnp
from jax import lax
from jax.experimental import pallas as pl
from jax.experimental.pallas import tpu as pltpu
from jax.sharding import PartitionSpec as P

MESH = pl.DeviceIdType.MESH
BF16, F32 = jnp.bfloat16, jnp.float32
NT = (((1,), (1,)), ((), ()))
TN = (((0,), (0,)), ((), ()))

TOK = 24
BOTH = 2 * TOK
CAP = 6
SLOTS = 8 * CAP
ROWS = 8 * SLOTS
HID = 192
WID = 512
COPIES = 127
HEAD = 32
CHUNKS = (((0, 384),), ((0, 256), (256, 384)))
AROUND = ((1, -1), (3, 1), (2, 2))
ALL = 8 * BOTH


def dot(a, b, dims=(((1,), (0,)), ((), ()))):
    return lax.dot_general(a, b, dims, preferred_element_type=F32)


def iota(shape, axis):
    return lax.broadcasted_iota(jnp.int32, shape, axis)


def kernel(
    tok1, gat1, exp1, tok2, gat2, exp2, gate_w, up_w, down_w,
    out1, out2,
    TV, GV, EV, ZT, IG, SM, YS, TK, WO, WA, WB, DW, PS, PR, PO, HT, OA, OS, OB, CM, ZF, ZS, ZR,
    ssem, rsem, lsem,
):
    e, d = lax.axis_index("expert"), lax.axis_index("dp")
    zh, x = d // 4, lax.rem(d, 4)
    zl, i8 = e // 8, lax.rem(e, 8)
    z = zh * 8 + zl
    ql = zl // 4
    q = zh * 2 + ql
    xa, xb, xc = x + 1 - 2 * lax.rem(x, 2), 3 - x, lax.rem(x + 2, 4)

    def at_z(step):
        other = lax.rem(z + step + 16, 16)
        return (lax.rem(other, 8) * 8 + i8, (other // 8) * 4 + x)

    def at_zl(step):
        return (lax.rem(zl + step + 8, 8) * 8 + i8, d)

    def at_x(place):
        return (e, zh * 4 + place)

    def at_yc(step):
        return (zl * 8 + lax.rem(i8 + step + 8, 8), d)

    barrier = pltpu.get_barrier_semaphore()
    greeted = (
        [at_z(k) for k in range(1, 16)]
        + [at_x(place) for place in (xa, xb, xc)]
        + [at_yc(k) for k in range(1, 8)]
    )
    for who in greeted:
        pl.semaphore_signal(barrier, inc=1, device_id=who, device_id_type=MESH)

    local = []

    def fetch(src, dst):
        copy = pltpu.make_async_copy(src, dst, lsem.at[len(local)])
        copy.start()
        local.append(copy)

    def columns(half, owner):
        return pl.ds(pl.multiple_of(half * 2048 + owner * WID, WID), WID)

    for n, (tok, gat, exp) in enumerate(((tok1, gat1, exp1), (tok2, gat2, exp2))):
        fetch(tok, TV.at[n])
        fetch(gat, GV.at[n])
        fetch(exp, EV.at[n])
    for m, cols in enumerate((columns(0, xa), columns(0, x), columns(1, x), columns(1, xb))):
        for n, w in enumerate((gate_w, up_w)):
            fetch(w.at[0, :, cols], WO.at[pl.ds(n * HID, HID), pl.ds(m * WID, WID)])
    fetch(down_w.at[0], DW)

    copies = []

    def send(src, dst, who):
        n = len(copies)
        copy = pltpu.make_async_remote_copy(
            src_ref=src,
            dst_ref=dst,
            send_sem=ssem.at[n],
            recv_sem=rsem.at[n],
            device_id=who,
            device_id_type=MESH,
        )
        copy.start()
        copies.append(copy)
        return copy

    for copy in local[:6]:
        copy.wait()
    ZT[0, q] = jnp.concatenate([TV[0].astype(F32), TV[1].astype(F32)], axis=0).astype(BF16)
    label = iota((128, TOK), 0)
    unit = jnp.where(iota((128, 128), 0) == iota((128, 128), 1), 1.0, 0.0).astype(BF16)
    tables = []
    for s in range(2):
        gates, experts = GV[s], EV[s]
        table = jnp.zeros((128, TOK), F32)
        for k in range(8):
            hit = lax.rem(label, 64) == experts[k : k + 1]
            table = jnp.where(hit, gates[k : k + 1], table)
        high = table.astype(BF16).astype(F32)
        tables.append(dot(jnp.where(label < 64, high, table - high).astype(BF16), unit, TN))
    IG[0, ql] = jnp.concatenate(tables, axis=0).astype(BF16)

    pl.semaphore_wait(barrier, len(greeted))

    parts = (pl.ds(0, HEAD), pl.ds(HEAD, BOTH - HEAD))
    first, second, table_second = {}, ([], []), []

    def spread(n, a):
        block = lax.rem(q - a + 4, 4)
        for b, step in AROUND:
            src = ZT.at[0, block, parts[n]]
            second[n].append(send(src, ZT.at[b, block, parts[n]], at_z(step)))

    table_first = send(IG.at[0, ql], IG.at[0, ql], at_z(4))
    for a in (2, 1, 3):
        first[0, a] = send(ZT.at[0, q, parts[0]], ZT.at[0, q, parts[0]], at_z(4 * a))
    spread(0, 0)
    table_first.wait_recv()
    table_second += [send(IG.at[0], IG.at[b], at_z(step)) for b, step in AROUND]
    for a in (1, 3):
        first[0, a].wait_recv()
        spread(0, a)
    for a in (2, 1, 3):
        first[1, a] = send(ZT.at[0, q, parts[1]], ZT.at[0, q, parts[1]], at_z(4 * a))
    first[0, 2].wait_recv()
    spread(0, 2)
    spread(1, 0)
    weights = []
    for cols, buffer, place in (
        ((columns(1, xa), columns(1, xc)), WA, xa),
        ((columns(0, xc), columns(0, xb)), WB, xb),
    ):
        for m in range(2):
            for h, w in enumerate((gate_w, up_w)):
                dst = buffer.at[pl.ds(h * HID, HID), pl.ds(m * WID, WID)]
                weights.append(send(w.at[0, :, cols[m]], dst, at_x(place)))
    for a in (1, 3, 2):
        first[1, a].wait_recv()
        spread(1, a)

    rows, cols = iota((ALL, ALL), 0), iota((ALL, ALL), 1)
    block = rows // TOK == cols // TOK
    before = jnp.where(block & (rows < cols), 1.0, 0.0).astype(BF16)
    after = jnp.where(block & (cols < rows), 1.0, 0.0).astype(BF16)
    pick, lane = iota((128, 128), 0), iota((128, 128), 1)
    wanted = zl * 8 + lax.rem(i8 + pick, 8)
    picks = jnp.where(
        ((pick < 8) & (lane == wanted)) | ((pick >= 8) & (pick < 16) & (lane == wanted + 64)),
        1.0,
        0.0,
    ).astype(BF16)

    for copy in table_second:
        copy.wait_recv()
    info = IG[...].reshape(ALL, 128)
    chosen = dot(picks[:16], info, NT)
    taken = chosen > 0.0
    place = dot(jnp.where(taken, 1.0, 0.0).astype(BF16), before)
    token = iota((16, ALL), 1)
    slot = place.astype(jnp.int32) + token // BOTH * CAP
    step_of = lax.rem(token, BOTH) // TOK
    held_row, all_row = iota((8 * HEAD, ALL), 0), iota((8 * HEAD, ALL), 1)
    for s in range(2):
        aim = jnp.where(taken & (step_of == s), slot, -1).astype(F32)
        same = held_row // HEAD * BOTH + lax.rem(held_row, HEAD) + s * (BOTH - HEAD) == all_row
        aim = dot(aim.astype(BF16), jnp.where(same, 1.0, 0.0).astype(BF16), NT)
        for k in range(8):
            SM[s, k * SLOTS : (k + 1) * SLOTS] = jnp.where(
                iota((SLOTS, 8 * HEAD), 0).astype(F32) == aim[k : k + 1], 1.0, 0.0
            ).astype(BF16)
    dispatch = []

    def select(s):
        start = s * (BOTH - HEAD)
        for half in range(2):
            held = ZT[:, 2 * half : 2 * half + 2, start : start + HEAD].reshape(8 * HEAD, WID)
            YS[s, :, half * WID : (half + 1) * WID] = dot(SM[s], held).astype(BF16)
        TK[s, 0:SLOTS, WID : 3 * WID] = YS[s, 0:SLOTS]

    def deliver(s):
        sent = []
        for k in range(1, 8):
            group = pl.ds(k * SLOTS, SLOTS)
            sent.append(send(YS.at[s, group], TK.at[s, group, pl.ds(WID, 2 * WID)], at_yc(k)))
        dispatch.append(sent)

    for copy in second[0]:
        copy.wait_recv()
    select(0)
    deliver(0)

    gates = dot(info, picks, NT)
    count = dot(after, jnp.where(gates > 0.0, 1.0, 0.0).astype(BF16))
    base = (iota((ALL, 128), 0) // BOTH * CAP + iota((ALL, 128), 1) * SLOTS).astype(F32)
    target = jnp.where(gates > 0.0, count + base, -1.0)
    column = iota((8 * TOK, ROWS), 1).astype(F32)
    for s in range(2):
        part = lambda v: v.reshape(8, BOTH, 128)[:, s * TOK : (s + 1) * TOK].reshape(8 * TOK, 128)
        aim, value = part(target), part(gates)
        for n in range(2):
            total = jnp.zeros((8 * TOK, ROWS), F32)
            for k in range(8):
                hit = column == aim[:, k : k + 1]
                total = jnp.where(hit, value[:, 8 * n + k : 8 * n + k + 1], total)
            CM[s, n] = total.astype(BF16)

    for copy in second[1]:
        copy.wait_recv()
    select(1)

    shared = []

    def share(s):
        sent = []
        for group in range(4):
            for k in (2 * group, 2 * group + 1):
                if k > 0:
                    dispatch[s][k - 1].wait_recv()
            rows = pl.ds(2 * group * SLOTS, 2 * SLOTS)
            for m, to, who in ((1, 0, xa), (2, 3, xb)):
                src = TK.at[s, rows, pl.ds(m * WID, WID)]
                sent.append(send(src, TK.at[s, rows, pl.ds(to * WID, WID)], at_x(who)))
        shared.append(sent)

    partial, crossed, around, passed = {}, {}, {}, {}
    other = lax.rem(d + 4, 8)

    def sums(s):
        for copy in shared[s]:
            copy.wait_recv()
        if s == 0:
            for copy in weights:
                copy.wait_recv()
        for c in CHUNKS[s]:
            partial[s, c] = []
            lanes = pl.ds(c[0], c[1] - c[0])
            for n, (w, start, who) in enumerate(((WA, 2 * WID, xa), (WB, 0, xb))):
                rows = TK[s, c[0] : c[1], start : start + 2 * WID]
                PS[s, n, :, c[0] : c[1]] = dot(w[...], rows, NT).astype(BF16)
                partial[s, c].append(send(PS.at[s, n, :, lanes], PR.at[s, n, :, lanes], at_x(who)))
        if s == 0:
            for copy in local[6:]:
                copy.wait()
        PO[s] = dot(WO[...], TK[s], NT)

    def held(s, c, block):
        return HT.at[s, block, :, pl.ds(c[0], c[1] - c[0])]

    def move(s, c, block, who):
        return send(held(s, c, block), held(s, c, block), who)

    def hidden(s, c):
        for copy in partial[s, c]:
            copy.wait_recv()
        both = PO[s, :, c[0] : c[1]]
        for n in range(2):
            both = both + PR[s, n, :, c[0] : c[1]].astype(F32)
        gate, up = both[:HID], both[HID:]
        HT[s, d, :, c[0] : c[1]] = (gate / (1.0 + jnp.exp(-gate)) * up).astype(BF16)
        crossed[s, c] = move(s, c, d, at_z(8))

    def go_round(s, c):
        around[s, c] = [move(s, c, d, at_x(place)) for place in (xa, xb)]

    def relay(s, c):
        around[s, c][0].wait_recv()
        around[s, c].append(move(s, c, zh * 4 + xa, at_x(xb)))

    def pass_on(s, c):
        crossed[s, c].wait_recv()
        passed[s, c] = [move(s, c, other, at_x(place)) for place in (xa, xb)]

    def pass_relay(s, c):
        passed[s, c][1].wait_recv()
        passed[s, c].append(move(s, c, 4 - zh * 4 + xb, at_x(xa)))

    def add(s, c, start):
        @pl.loop(0, 4)
        def _(n):
            w = DW[pl.ds(pl.multiple_of((start + n) * HID, HID), HID), :]
            OA[s, c[0] : c[1]] += dot(HT[s, start + n, :, c[0] : c[1]], w, TN)

    def project_own(s, c):
        for copy in around[s, c][1:]:
            copy.wait_recv()
        OA[s, c[0] : c[1]] = jnp.zeros((c[1] - c[0], WID), F32)
        add(s, c, zh * 4)

    returned = ([], [])

    def project(s, c):
        for copy in (passed[s, c][0], passed[s, c][2]):
            copy.wait_recv()
        add(s, c, 4 - zh * 4)
        OS[s, c[0] : c[1]] = OA[s, c[0] : c[1]].astype(BF16)
        for k in range(c[0] // SLOTS, c[1] // SLOTS):
            group = pl.ds(k * SLOTS, SLOTS)
            if k == 0:
                OB[s, 0:SLOTS] = OS[s, 0:SLOTS]
            else:
                returned[s].append(send(OS.at[s, group], OB.at[s, group], at_yc(-k)))

    last = []

    def combine(s):
        for copy in returned[s]:
            copy.wait_recv()
        rows_in = OB[s]
        total = (dot(CM[s, 0], rows_in) + dot(CM[s, 1], rows_in)).reshape(8, TOK, WID)
        for n in range(4):
            ZF[s, :, n * TOK : (n + 1) * TOK] = total[:, :, n * 128 : (n + 1) * 128]
        ZS[s] = ZF[s].astype(BF16)
        sent = []
        for k in range(1, 8):
            block = k % 4 * 2 + lax.rem(zl + k, 8) // 4
            sent.append(send(ZS.at[s, block], ZR.at[s, k], at_zl(k)))
        last.append(sent)

    def finish(s, out):
        for copy in last[s]:
            copy.wait_recv()
        total = ZF[s, ql]
        for k in range(1, 8):
            total = total + ZR[s, k].astype(F32)
        for n in range(4):
            out[:, n * 128 : (n + 1) * 128] = total[n * TOK : (n + 1) * TOK].astype(BF16)

    (one,), (two, three) = CHUNKS
    share(0)
    deliver(1)
    sums(0)
    share(1)
    hidden(0, one)
    go_round(0, one)
    sums(1)
    relay(0, one)
    hidden(1, two)
    go_round(1, two)
    hidden(1, three)
    go_round(1, three)
    pass_on(0, one)
    relay(1, two)
    relay(1, three)
    project_own(0, one)
    pass_relay(0, one)
    project(0, one)
    pass_on(1, two)
    pass_on(1, three)
    combine(0)
    pass_relay(1, two)
    project_own(1, two)
    project_own(1, three)
    pass_relay(1, three)
    project(1, two)
    project(1, three)
    combine(1)
    finish(0, out1)
    finish(1, out2)
    for copy in copies:
        copy.wait_send()
    assert len(copies) == COPIES


def body(tok1, gat1, exp1, tok2, gat2, exp2, gate_w, up_w, down_w):
    vmem = pl.BlockSpec(memory_space=pltpu.VMEM)
    hbm = pl.BlockSpec(memory_space=pl.ANY)
    scratch = [
        pltpu.VMEM((2, TOK, WID), BF16),
        pltpu.VMEM((2, 8, TOK), F32),
        pltpu.VMEM((2, 8, TOK), jnp.int32),
        pltpu.VMEM((4, 4, BOTH, WID), BF16),
        pltpu.VMEM((4, 2, BOTH, 128), BF16),
        pltpu.VMEM((2, ROWS, 8 * HEAD), BF16),
        pltpu.VMEM((2, ROWS, 2 * WID), BF16),
        pltpu.VMEM((2, ROWS, 4 * WID), BF16),
        pltpu.VMEM((2 * HID, 4 * WID), BF16),
        pltpu.VMEM((2 * HID, 2 * WID), BF16),
        pltpu.VMEM((2 * HID, 2 * WID), BF16),
        pltpu.VMEM((8 * HID, WID), BF16),
        pltpu.VMEM((2, 2, 2 * HID, ROWS), BF16),
        pltpu.VMEM((2, 2, 2 * HID, ROWS), BF16),
        pltpu.VMEM((2, 2 * HID, ROWS), F32),
        pltpu.VMEM((2, 8, HID, ROWS), BF16),
        pltpu.VMEM((2, ROWS, WID), F32),
        pltpu.VMEM((2, ROWS, WID), BF16),
        pltpu.VMEM((2, ROWS, WID), BF16),
        pltpu.VMEM((2, 2, 8 * TOK, ROWS), BF16),
        pltpu.VMEM((2, 8, 4 * TOK, 128), F32),
        pltpu.VMEM((2, 8, 4 * TOK, 128), BF16),
        pltpu.VMEM((2, 8, 4 * TOK, 128), BF16),
        pltpu.SemaphoreType.DMA((COPIES,)),
        pltpu.SemaphoreType.DMA((COPIES,)),
        pltpu.SemaphoreType.DMA((15,)),
    ]
    result = jax.ShapeDtypeStruct((TOK, WID), BF16)
    return pl.pallas_call(
        kernel,
        out_shape=(result, result),
        in_specs=[hbm] * 9,
        out_specs=(vmem, vmem),
        scratch_shapes=scratch,
        compiler_params=pltpu.CompilerParams(
            collective_id=0, has_side_effects=True, vmem_limit_bytes=60 * 2**20
        ),
        cost_estimate=pl.CostEstimate(
            flops=2 * 2 * ROWS * (2 * HID * 4096 + 1536 * WID),
            bytes_accessed=3 * HID * 4096 * 2,
            transcendentals=2 * HID * ROWS,
        ),
        name="moe",
    )(tok1, gat1.T, exp1.T, tok2, gat2.T, exp2.T, gate_w, up_w, down_w)


def solution(mesh):
    return jax.shard_map(
        body,
        mesh=mesh,
        in_specs=(
            P("expert", "dp"),
            P("expert", None),
            P("expert", None),
            P("expert", "dp"),
            P("expert", None),
            P("expert", None),
            P("expert", "dp", None),
            P("expert", "dp", None),
            P("expert", None, "dp"),
        ),
        out_specs=(P("expert", "dp"), P("expert", "dp")),
        check_vma=False,
    )
```
